32 devices in a mesh: src: 4 (over y, core), tgt: 8 (over z, x).
Axes of the slice: x: 2, y: 2, z: 4, core: 2. Of those that a mesh axis runs over, the one named last changes fastest.
Arguments:
- noise: float32 [4096, 384], P(('src', 'tgt')), may hold values from -16 to 16
- data: float32 [8192, 384], P('tgt', 'src'), may hold values from -6 to 6
Outputs:
- velocity: float32 [4096, 384], P(('src', 'tgt'))
- target_potential: float32 [8192], P('tgt')
The draws below stay inside these ranges and needn't reach their ends.
All inputs are finite; a program needn't handle non-finite values.
Results may differ from the reference program's by a relative error of at most 0.0003.
Values sent between devices are 32-bit elements; how exact they have to be, the bound alone decides.
A program may use at most 64 MiB of HBM per device.

```python
import math
import jax
import jax.numpy as jnp
from jax import lax

FEAT = 384
S_DEV = 1024
ITERS = 3
NS = 4096
NT = 8192


def draw_noise(key, part):
    base = jax.random.normal(jax.random.fold_in(key, 11), (NS, FEAT), jnp.float32)
    base = jnp.clip(base, -6.0, 6.0)
    return base


def level_of(rng, dims, pieces, smallest, high):
    gain, own = 1.0, jax.random.fold_in(rng, 6)
    for axis_at, blocks in pieces:
        draws = jnp.exp(jax.random.uniform(jax.random.fold_in(own, axis_at), (blocks,), jnp.float32, smallest / len(pieces), high / len(pieces)))
        gain = gain * jnp.repeat(draws, dims[axis_at] // blocks).reshape([-1 if axis == axis_at else 1 for axis in range(len(dims))])
    return gain


def gaussian(stream_key, extent, spread, reach, cuts=(), kind=jnp.bfloat16):
    entries = spread * jax.random.normal(stream_key, extent, jnp.float32)
    if cuts:
        entries = entries * level_of(stream_key, extent, cuts, -0.22, 0.18)
    return jnp.clip(entries, -reach, reach).astype(kind)


def setup_inputs(seed: int = 0) -> dict:
    streams_of = jax.random.split(jax.random.key(seed), 3)
    return {
        "noise": draw_noise(jax.random.fold_in(streams_of[2], 71), 0),
        "data": gaussian(streams_of[1], (NT, FEAT), 1.0, 6.0, ((0, 8), (1, 4)), jnp.float32),
    }


EPS = 0.05


def reference(noise, data):
    nblk = NS // S_DEV
    blocks = noise.reshape(nblk, S_DEV, FEAT)
    data_sq = jnp.sum(data * data, axis=1)

    def cost_of(rows):
        rows_sq = jnp.sum(rows * rows, axis=1)
        cross = jnp.dot(rows, data.T, precision=lax.Precision.HIGHEST, preferred_element_type=jnp.float32)
        return (rows_sq[:, None] + data_sq[None, :] - 2.0 * cross) / FEAT

    def row_lse(g_pot):
        def one(rows):
            z = (g_pot[None, :] - cost_of(rows)) / EPS
            top = jnp.max(z, axis=1)
            return top + jnp.log(jnp.sum(jnp.exp(z - top[:, None]), axis=1))
        return lax.map(one, blocks).reshape(NS)

    def col_lse(f_pot):
        f_blocks = f_pot.reshape(nblk, S_DEV)

        def step(carry, item):
            top, total = carry
            rows, f_part = item
            z = (f_part[:, None] - cost_of(rows)) / EPS
            local_top = jnp.max(z, axis=0)
            local_sum = jnp.sum(jnp.exp(z - local_top[None, :]), axis=0)
            new_top = jnp.maximum(top, local_top)
            total = total * jnp.exp(top - new_top) + local_sum * jnp.exp(local_top - new_top)
            return (new_top, total), None

        init = (jnp.full((NT,), -jnp.inf, dtype=jnp.float32), jnp.zeros((NT,), jnp.float32))
        (top, total), _ = lax.scan(step, init, (blocks, f_blocks))
        return top + jnp.log(total)

    g_pot = jnp.zeros((NT,), jnp.float32)
    for step_index in range(ITERS):
        f_pot = -EPS * (math.log(NS) + row_lse(g_pot))
        g_pot = -EPS * (math.log(NT) + col_lse(f_pot))

    def final(rows):
        z = (g_pot[None, :] - cost_of(rows)) / EPS
        top = jnp.max(z, axis=1)
        lrow = top + jnp.log(jnp.sum(jnp.exp(z - top[:, None]), axis=1))
        weight = jnp.exp(z - lrow[:, None])
        return jnp.dot(weight, data, precision=lax.Precision.HIGHEST, preferred_element_type=jnp.float32)

    bary = lax.map(final, blocks).reshape(NS, FEAT)
    return bary - noise, g_pot
```

```python
import functools
import math

import jax
import jax.numpy as jnp
from jax import lax
from jax.experimental import pallas as pl
from jax.experimental.pallas import tpu as pltpu
from jax.sharding import PartitionSpec as P

ITERS = 3
EPS = 0.05
LOG2E = 1.0 / math.log(2.0)
LANES = 128
MESH = pl.DeviceIdType.MESH


def split(value):
    high = value.astype(jnp.bfloat16)
    return high, (value - high.astype(jnp.float32)).astype(jnp.bfloat16)


def kernel(n_s, n_t, noise_ref, data_ref, vel_ref, pot_ref, src_all, tgt_all, tgt_hi, tgt_lo, tile, col, bary,
           row_pair, col_pair, row_sum, col_sum, from_x, to_z, from_z,
           src_ss, src_rs, src_fs, src_fr, tgt_ss, tgt_rs, tgt_fs, tgt_fr,
           rp_s, rp_r, cp_s, cp_r, rs_s, rs_r, cs_s, cs_r, ax_s, ax_r, bz_s, bz_r):
    s_me, t_me = lax.axis_index("src"), lax.axis_index("tgt")
    rows_own, feat = noise_ref.shape
    feat_own = data_ref.shape[1]
    n_rows, n_cols = tile.shape
    row_chunks, col_chunks = n_rows // LANES, n_cols // LANES
    src_total, tgt_total = n_rows * n_s, n_cols * n_t
    halves_t = n_t // 2
    f32 = jnp.float32

    def on_tgt(peer):
        return (s_me, peer)

    def on_src(peer):
        return (peer, t_me)

    barrier = pltpu.get_barrier_semaphore()
    for off in range(1, n_t):
        pl.semaphore_signal(barrier, 1, device_id=on_tgt(lax.rem(t_me + off, n_t)), device_id_type=MESH)
    for off in range(1, n_s):
        pl.semaphore_signal(barrier, 1, device_id=on_src(lax.rem(s_me + off, n_s)), device_id_type=MESH)
    tgt_all[pl.ds(pl.multiple_of(s_me * feat_own, 8), feat_own), :] = data_ref[...].T
    src_all[pl.ds(pl.multiple_of(t_me * rows_own, 8), rows_own), :] = noise_ref[...]
    pl.semaphore_wait(barrier, n_t + n_s - 2)

    def remote(ref, where, dst, send, recv, dev):
        return pltpu.make_async_remote_copy(
            src_ref=ref.at[where], dst_ref=dst, send_sem=send, recv_sem=recv, device_id=dev, device_id_type=MESH)

    def gather_ops(buf, rows, n, me, dev_of, ss, rs, fs, fr):
        hi, lo = me // 2, lax.rem(me, 2)
        nh = n // 2

        def block(idx):
            return buf.at[pl.ds(pl.multiple_of(idx * rows, 8), rows), :]

        def far(h, owner):
            return pltpu.make_async_remote_copy(
                src_ref=block(owner), dst_ref=block(owner), send_sem=ss.at[h], recv_sem=rs.at[owner // 2],
                device_id=dev_of(h * 2 + lo), device_id_type=MESH)

        def near(owner, h):
            return pltpu.make_async_remote_copy(
                src_ref=block(owner), dst_ref=block(owner), send_sem=fs.at[h], recv_sem=fr.at[h],
                device_id=dev_of(hi * 2 + 1 - lo), device_id_type=MESH)

        offs = list(range(1, nh))

        def begin():
            for off in offs:
                far(lax.rem(hi + off, nh), me).start()
            near(me, hi).start()

        def forward():
            for off in offs:
                h = lax.rem(hi + off, nh)
                far(h, h * 2 + lo).wait_recv()
                near(h * 2 + lo, h).start()

        def finish():
            for off in [0] + offs:
                h = lax.rem(hi + off, nh)
                near(h * 2 + 1 - lo, h).wait_recv()

        def drain():
            for off in offs:
                far(lax.rem(hi + off, nh), me).wait_send()
            for off in [0] + offs:
                h = lax.rem(hi + off, nh)
                near(h * 2 + lo, h).wait_send()

        return begin, forward, finish, drain

    g_src = gather_ops(src_all, rows_own, n_t, t_me, on_tgt, src_ss, src_rs, src_fs, src_fr)
    g_tgt = gather_ops(tgt_all, feat_own, n_s, s_me, on_src, tgt_ss, tgt_rs, tgt_fs, tgt_fr)
    g_src[0]()
    g_tgt[0]()
    g_tgt[1]()
    g_src[1]()
    g_tgt[2]()

    def exchange(buf, n, me, dev_of, ss, rs):
        def op(peer, owner):
            return pltpu.make_async_remote_copy(
                src_ref=buf.at[owner], dst_ref=buf.at[owner], send_sem=ss.at[peer], recv_sem=rs.at[owner],
                device_id=dev_of(peer), device_id_type=MESH)

        def start():
            for off in range(1, n):
                op(lax.rem(me + off, n), me).start()

        def wait():
            for off in range(1, n):
                peer = lax.rem(me + off, n)
                op(peer, peer).wait_recv()

        def drain():
            for off in range(1, n):
                op(lax.rem(me + off, n), me).wait_send()

        return start, wait, drain

    x_rp = exchange(row_pair, n_t, t_me, on_tgt, rp_s, rp_r)
    x_cp = exchange(col_pair, n_s, s_me, on_src, cp_s, cp_r)
    x_rs = [exchange(row_sum.at[k], n_t, t_me, on_tgt, rs_s.at[k], rs_r.at[k]) for k in range(ITERS)]
    x_cs = [exchange(col_sum.at[k], n_s, s_me, on_src, cs_s.at[k], cs_r.at[k]) for k in range(ITERS - 1)]

    scale = LOG2E / (feat * EPS)
    t_hi, t_lo = split(tgt_all[...])
    tgt_hi[...] = t_hi
    tgt_lo[...] = t_lo
    g_src[2]()
    source = src_all[...]
    source_sq = jnp.broadcast_to(jnp.sum(source * source, axis=1, keepdims=True), (n_rows, LANES))
    col[...] = source_sq
    s_hi, s_lo = split(source)
    width = 2 * LANES

    def cost_step(k, carry):
        cols = pl.ds(pl.multiple_of(k * width, width), width)
        w_hi, w_lo = tgt_hi[:, cols], tgt_lo[:, cols]
        cross = jnp.dot(s_hi, w_hi, preferred_element_type=f32)
        cross += jnp.dot(s_hi, w_lo, preferred_element_type=f32)
        cross += jnp.dot(s_lo, w_hi, preferred_element_type=f32)
        block = tgt_all[:, cols]
        target_sq = jnp.sum(block * block, axis=0, keepdims=True)
        both = jnp.concatenate([col[...], col[...]], axis=1)
        tile[:, cols] = (both + target_sq - 2.0 * cross) * scale
        return carry

    lax.fori_loop(0, n_cols // width, cost_step, 0)

    def rows_of(c):
        return slice(c * LANES, (c + 1) * LANES)

    for c in range(row_chunks):
        top = -tile[rows_of(c), rows_of(0)]
        for k in range(1, col_chunks):
            top = jnp.maximum(top, -tile[rows_of(c), rows_of(k)])
        total = jnp.zeros_like(top)
        for k in range(col_chunks):
            total += jnp.exp2(-tile[rows_of(c), rows_of(k)] - top)
        top, total = top.T, total.T
        best = jnp.max(top, axis=0, keepdims=True)
        row_pair[t_me, c:c + 1, :] = best
        row_pair[t_me, row_chunks + c:row_chunks + c + 1, :] = jnp.sum(
            total * jnp.exp2(top - best), axis=0, keepdims=True)
    x_rp[0]()
    x_rp[1]()

    def merge(buf, n, chunks):
        best = buf[0, :chunks, :]
        for d in range(1, n):
            best = jnp.maximum(best, buf[d, :chunks, :])
        total = jnp.zeros_like(best)
        for d in range(n):
            total += buf[d, chunks:, :] * jnp.exp2(buf[d, :chunks, :] - best)
        return best + jnp.log(total) * LOG2E

    def to_col(packed):
        for c in range(row_chunks):
            col[rows_of(c), :] = jnp.broadcast_to(packed[c:c + 1, :], (LANES, LANES)).T

    f_pot = -(math.log2(src_total) + merge(row_pair, n_t, row_chunks))
    to_col(f_pot)

    tops = []
    for k in range(col_chunks):
        def top_step(c, best, k=k):
            rows = pl.ds(pl.multiple_of(c * LANES, LANES), LANES)
            z = col[rows, :] - tile[rows, rows_of(k)]
            return jnp.maximum(best, jnp.max(z.reshape(LANES // 8, 8, LANES), axis=0))

        best = lax.fori_loop(0, row_chunks, top_step, jnp.full((8, LANES), -jnp.inf, f32), unroll=True)
        best = jnp.max(best, axis=0, keepdims=True)
        tops.append(best)

        def exp_step(c, total, k=k, best=best):
            rows = pl.ds(pl.multiple_of(c * LANES, LANES), LANES)
            e = jnp.exp2(col[rows, :] - tile[rows, rows_of(k)] - best)
            tile[rows, rows_of(k)] = e
            return total + jnp.sum(e.reshape(LANES // 8, 8, LANES), axis=0)

        total = lax.fori_loop(0, row_chunks, exp_step, jnp.zeros((8, LANES), f32), unroll=True)
        col_pair[s_me, k:k + 1, :] = best
        col_pair[s_me, col_chunks + k:col_chunks + k + 1, :] = jnp.sum(total, axis=0, keepdims=True)
    x_cp[0]()
    x_cp[1]()
    g_first = -(math.log2(tgt_total) + merge(col_pair, n_s, col_chunks))
    base = jnp.exp2(jnp.concatenate(tops, axis=0) + g_first)
    b = base

    def row_products(slot, b):
        for c in range(row_chunks):
            total = tile[rows_of(c), rows_of(0)] * b[0:1, :]
            for k in range(1, col_chunks):
                total += tile[rows_of(c), rows_of(k)] * b[k:k + 1, :]
            row_sum[slot, t_me, c:c + 1, :] = jnp.sum(total.T, axis=0, keepdims=True)

    def add_up(buf, slot, n):
        total = buf[slot, 0]
        for d in range(1, n):
            total += buf[slot, d]
        return total

    for it in range(ITERS - 1):
        row_products(it, b)
        x_rs[it][0]()
        x_rs[it][1]()
        to_col(1.0 / (src_total * add_up(row_sum, it, n_t)))
        for k in range(col_chunks):
            total = jnp.zeros((8, LANES), f32)
            for c in range(row_chunks):
                e = tile[rows_of(c), rows_of(k)] * col[rows_of(c), :]
                total += jnp.sum(e.reshape(LANES // 8, 8, LANES), axis=0)
            col_sum[it, s_me, k:k + 1, :] = jnp.sum(total, axis=0, keepdims=True) * base[k:k + 1, :]
        x_cs[it][0]()
        x_cs[it][1]()
        beta = 1.0 / (tgt_total * add_up(col_sum, it, n_s))
        b = base * beta
    pot_ref[...] = EPS * (g_first * math.log(2.0) + jnp.log(beta))

    last = ITERS - 1
    row_products(last, b)
    x_rs[last][0]()
    for k in range(col_chunks):
        t_hi, t_lo = split(tgt_all[:, rows_of(k)] * b[k:k + 1, :])
        tgt_hi[:, rows_of(k)] = t_hi
        tgt_lo[:, rows_of(k)] = t_lo

    h_me, l_me = t_me // 2, lax.rem(t_me, 2)
    pair = 2 * rows_own
    dims = (((1,), (1,)), ((), ()))

    def send_x(h, lo):
        return pltpu.make_async_remote_copy(
            src_ref=bary.at[pl.ds(pl.multiple_of((h * 2 + lo) * rows_own, 8), rows_own), :], dst_ref=from_x.at[h],
            send_sem=ax_s.at[h], recv_sem=ax_r.at[h], device_id=on_tgt(h_me * 2 + 1 - l_me), device_id_type=MESH)

    def send_z(h, sender):
        return pltpu.make_async_remote_copy(
            src_ref=to_z.at[h], dst_ref=from_z.at[sender], send_sem=bz_s.at[h], recv_sem=bz_r.at[sender],
            device_id=on_tgt(h * 2 + l_me), device_id_type=MESH)

    def own_rows(h):
        return bary[pl.ds(pl.multiple_of((h * 2 + l_me) * rows_own, 8), rows_own), :]

    def compute(h):
        rows = pl.ds(pl.multiple_of(h * pair, 16), pair)
        e_hi, e_lo = split(tile[rows, :])
        out = lax.dot_general(e_hi, tgt_hi[...], dims, preferred_element_type=f32)
        out += lax.dot_general(e_hi, tgt_lo[...], dims, preferred_element_type=f32)
        out += lax.dot_general(e_lo, tgt_hi[...], dims, preferred_element_type=f32)
        bary[rows, :] = out
        send_x(h, 1 - l_me).start()

    def pass_on(h):
        send_x(h, 1 - l_me).wait_recv()
        to_z[h] = own_rows(h) + from_x[h]
        send_z(h, h_me).start()

    def step(off, carry):
        compute(lax.rem(h_me + off, halves_t))

        @pl.when(off > 1)
        def _():
            pass_on(lax.rem(h_me + off - 1, halves_t))

        return carry

    lax.fori_loop(1, halves_t + 1, step, 0)
    x_rs[last][1]()
    to_col(1.0 / add_up(row_sum, last, n_t))
    send_x(h_me, 1 - l_me).wait_recv()
    total = own_rows(h_me) + from_x[h_me]
    for off in range(1, halves_t):
        h = lax.rem(h_me + off, halves_t)
        send_z(h, h).wait_recv()
        total += from_z[h]
    inv = col[pl.ds(pl.multiple_of(t_me * rows_own, 8), rows_own), :]
    inv = jnp.concatenate([inv] * (feat // LANES), axis=1)
    vel_ref[...] = total * inv - noise_ref[...]

    g_src[3]()
    g_tgt[3]()
    for ops in [x_rp, x_cp] + x_rs + x_cs:
        ops[2]()
    for off in range(1, halves_t):
        h = lax.rem(h_me + off, halves_t)
        send_x(h, 1 - l_me).wait_send()
        send_z(h, h_me).wait_send()
    send_x(h_me, 1 - l_me).wait_send()


def per_device(n_s, n_t, noise, data):
    rows_own, feat = noise.shape
    n_rows, n_cols = rows_own * n_t, data.shape[0]
    rc, cc = n_rows // LANES, n_cols // LANES
    nh, nhs = n_t // 2, n_s // 2
    f32, bf16 = jnp.float32, jnp.bfloat16
    vmem = pltpu.VMEM
    dma = pltpu.SemaphoreType.DMA
    vel, pot = pl.pallas_call(
        functools.partial(kernel, n_s, n_t),
        out_shape=(jax.ShapeDtypeStruct((rows_own, feat), f32), jax.ShapeDtypeStruct((cc, LANES), f32)),
        in_specs=[pl.BlockSpec(memory_space=vmem)] * 2,
        out_specs=(pl.BlockSpec(memory_space=vmem), pl.BlockSpec(memory_space=vmem)),
        scratch_shapes=[
            vmem((n_rows, feat), f32), vmem((feat, n_cols), f32),
            vmem((feat, n_cols), bf16), vmem((feat, n_cols), bf16),
            vmem((n_rows, n_cols), f32), vmem((n_rows, LANES), f32), vmem((n_rows, feat), f32),
            vmem((n_t, 2 * rc, LANES), f32), vmem((n_s, 2 * cc, LANES), f32),
            vmem((ITERS, n_t, rc, LANES), f32), vmem((ITERS - 1, n_s, cc, LANES), f32),
            vmem((nh, rows_own, feat), f32), vmem((nh, rows_own, feat), f32), vmem((nh, rows_own, feat), f32),
            dma((nh,)), dma((nh,)), dma((nh,)), dma((nh,)),
            dma((nhs,)), dma((nhs,)), dma((nhs,)), dma((nhs,)),
            dma((n_t,)), dma((n_t,)), dma((n_s,)), dma((n_s,)),
            dma((ITERS, n_t)), dma((ITERS, n_t)), dma((ITERS - 1, n_s)), dma((ITERS - 1, n_s)),
            dma((nh,)), dma((nh,)), dma((nh,)), dma((nh,)),
        ],
        compiler_params=pltpu.CompilerParams(
            collective_id=0, has_side_effects=True, vmem_limit_bytes=48 * 1024 * 1024),
    )(noise, data)
    return vel, pot.reshape(n_cols)


def solution(mesh):
    return jax.shard_map(
        functools.partial(per_device, mesh.shape["src"], mesh.shape["tgt"]),
        mesh=mesh,
        in_specs=(P(("src", "tgt"), None), P("tgt", "src")),
        out_specs=(P(("src", "tgt"), None), P("tgt")),
        check_vma=False,
    )
```

```python
import functools
import math

import jax
import jax.numpy as jnp
from jax import lax
from jax.experimental import pallas as pl
from jax.experimental.pallas import tpu as pltpu
from jax.sharding import PartitionSpec as P

ITERS = 3
EPS = 0.05
LOG2E = 1.0 / math.log(2.0)
LANES = 128
MESH = pl.DeviceIdType.MESH


def split(value):
    high = value.astype(jnp.bfloat16)
    return high, (value - high.astype(jnp.float32)).astype(jnp.bfloat16)


def kernel(n_s, n_t, noise_ref, data_ref, vel_ref, pot_ref, src_all, tgt_all, tgt_hi, tgt_lo, tile, col, bary,
           row_pair, col_pair, row_sum, col_sum, from_x, to_z, from_z,
           src_us, src_ds, src_rs, src_fs, src_fr, tgt_ss, tgt_rs, tgt_fs, tgt_fr,
           rp_s, rp_r, cp_s, cp_r, rs_s, rs_r, cs_s, cs_r, ax_s, ax_r, bz_s, bz_r):
    s_me, t_me = lax.axis_index("src"), lax.axis_index("tgt")
    rows_own, feat = noise_ref.shape
    feat_own = data_ref.shape[1]
    n_rows, n_cols = tile.shape
    row_chunks, col_chunks = n_rows // LANES, n_cols // LANES
    src_total, tgt_total = n_rows * n_s, n_cols * n_t
    halves_t = n_t // 2
    f32 = jnp.float32

    def on_tgt(peer):
        return (s_me, peer)

    def on_src(peer):
        return (peer, t_me)

    barrier = pltpu.get_barrier_semaphore()
    for off in range(1, n_t):
        pl.semaphore_signal(barrier, 1, device_id=on_tgt(lax.rem(t_me + off, n_t)), device_id_type=MESH)
    for off in range(1, n_s):
        pl.semaphore_signal(barrier, 1, device_id=on_src(lax.rem(s_me + off, n_s)), device_id_type=MESH)
    tgt_all[pl.ds(pl.multiple_of(s_me * feat_own, 8), feat_own), :] = data_ref[...].T
    src_all[pl.ds(pl.multiple_of(t_me * rows_own, 8), rows_own), :] = noise_ref[...]
    pl.semaphore_wait(barrier, n_t + n_s - 2)

    def gather_ops(buf, rows, n, me, dev_of, ss, rs, fs, fr):
        hi, lo = me // 2, lax.rem(me, 2)
        nh = n // 2

        def block(idx):
            return buf.at[pl.ds(pl.multiple_of(idx * rows, 8), rows), :]

        def far(h, owner):
            return pltpu.make_async_remote_copy(
                src_ref=block(owner), dst_ref=block(owner), send_sem=ss.at[h], recv_sem=rs.at[owner // 2],
                device_id=dev_of(h * 2 + lo), device_id_type=MESH)

        def near(owner, h):
            return pltpu.make_async_remote_copy(
                src_ref=block(owner), dst_ref=block(owner), send_sem=fs.at[h], recv_sem=fr.at[h],
                device_id=dev_of(hi * 2 + 1 - lo), device_id_type=MESH)

        offs = list(range(1, nh))

        def begin():
            for off in offs:
                far(lax.rem(hi + off, nh), me).start()
            near(me, hi).start()

        def forward():
            for off in offs:
                h = lax.rem(hi + off, nh)
                far(h, h * 2 + lo).wait_recv()
                near(h * 2 + lo, h).start()

        def finish():
            for off in [0] + offs:
                h = lax.rem(hi + off, nh)
                near(h * 2 + 1 - lo, h).wait_recv()

        def drain():
            for off in offs:
                far(lax.rem(hi + off, nh), me).wait_send()
            for off in [0] + offs:
                h = lax.rem(hi + off, nh)
                near(h * 2 + lo, h).wait_send()

        return begin, forward, finish, drain

    h_me, l_me = t_me // 2, lax.rem(t_me, 2)
    partner = h_me * 2 + 1 - l_me

    def src_copy(h, low, send, recv, dev):
        ref = src_all.at[pl.ds(pl.multiple_of((h * 2 + low) * rows_own, 8), rows_own), :]
        return pltpu.make_async_remote_copy(
            src_ref=ref, dst_ref=ref, send_sem=send.at[h], recv_sem=recv.at[h],
            device_id=on_tgt(dev), device_id_type=MESH)

    def up(h):
        return src_copy(h, l_me, src_us, src_rs, t_me + 2)

    def down(h):
        return src_copy(h, l_me, src_ds, src_rs, t_me - 2)

    def near(h):
        return src_copy(h, l_me, src_fs, src_fr, partner)

    def send_on(h, go_up, go_down):
        if go_up:
            @pl.when(h_me < halves_t - 1)
            def _():
                up(h).start()
        if go_down:
            @pl.when(h_me > 0)
            def _():
                down(h).start()
        near(h).start()

    def forward(k):
        @pl.when(h_me - k >= 0)
        def _():
            src_copy(h_me - k, l_me, src_us, src_rs, partner).wait_recv()
            send_on(h_me - k, True, False)

        @pl.when(h_me + k < halves_t)
        def _():
            src_copy(h_me + k, l_me, src_ds, src_rs, partner).wait_recv()
            send_on(h_me + k, False, True)

    def drain_src():
        for h in range(halves_t):
            @pl.when(jnp.logical_and(h <= h_me, h_me < halves_t - 1))
            def _(h=h):
                up(h).wait_send()

            @pl.when(jnp.logical_and(h >= h_me, h_me > 0))
            def _(h=h):
                down(h).wait_send()

            near(h).wait_send()

    g_tgt = gather_ops(tgt_all, feat_own, n_s, s_me, on_src, tgt_ss, tgt_rs, tgt_fs, tgt_fr)
    send_on(h_me, True, True)
    g_tgt[0]()
    forward(1)
    g_tgt[1]()
    forward(2)
    g_tgt[2]()

    def exchange(buf, n, me, dev_of, ss, rs):
        def op(peer, owner):
            return pltpu.make_async_remote_copy(
                src_ref=buf.at[owner], dst_ref=buf.at[owner], send_sem=ss.at[peer], recv_sem=rs.at[owner],
                device_id=dev_of(peer), device_id_type=MESH)

        def start():
            for off in range(1, n):
                op(lax.rem(me + off, n), me).start()

        def wait():
            for off in range(1, n):
                peer = lax.rem(me + off, n)
                op(peer, peer).wait_recv()

        def drain():
            for off in range(1, n):
                op(lax.rem(me + off, n), me).wait_send()

        return start, wait, drain

    x_rp = exchange(row_pair, n_t, t_me, on_tgt, rp_s, rp_r)
    x_cp = exchange(col_pair, n_s, s_me, on_src, cp_s, cp_r)
    x_rs = [exchange(row_sum.at[k], n_t, t_me, on_tgt, rs_s.at[k], rs_r.at[k]) for k in range(ITERS)]
    x_cs = [exchange(col_sum.at[k], n_s, s_me, on_src, cs_s.at[k], cs_r.at[k]) for k in range(ITERS - 1)]

    scale = LOG2E / (feat * EPS)
    t_hi, t_lo = split(tgt_all[...])
    tgt_hi[...] = t_hi
    tgt_lo[...] = t_lo
    target_sq = jnp.sum(tgt_all[...] * tgt_all[...], axis=0, keepdims=True)
    pair = 2 * rows_own

    def rows_of(c):
        return slice(c * LANES, (c + 1) * LANES)

    def first_row_sums(c):
        rows = pl.ds(pl.multiple_of(c * LANES, LANES), LANES)
        top = -tile[rows, rows_of(0)]
        for k in range(1, col_chunks):
            top = jnp.maximum(top, -tile[rows, rows_of(k)])
        total = jnp.zeros_like(top)
        for k in range(col_chunks):
            total += jnp.exp2(-tile[rows, rows_of(k)] - top)
        top, total = top.T, total.T
        best = jnp.max(top, axis=0, keepdims=True)
        row_pair[t_me, pl.ds(c, 1), :] = best
        row_pair[t_me, pl.ds(row_chunks + c, 1), :] = jnp.sum(total * jnp.exp2(top - best), axis=0, keepdims=True)

    def cost_rows(h):
        src_copy(h, 1 - l_me, src_fs, src_fr, partner).wait_recv()
        rows = pl.ds(pl.multiple_of(h * pair, 16), pair)
        source = src_all[rows, :]
        source_sq = jnp.sum(source * source, axis=1, keepdims=True)
        s_hi, s_lo = split(source)
        cross = jnp.dot(s_hi, tgt_hi[...], preferred_element_type=f32)
        cross += jnp.dot(s_hi, tgt_lo[...], preferred_element_type=f32)
        cross += jnp.dot(s_lo, tgt_hi[...], preferred_element_type=f32)
        tile[rows, :] = (source_sq + target_sq - 2.0 * cross) * scale
        if pair % LANES == 0:
            for c in range(pair // LANES):
                first_row_sums(h * (pair // LANES) + c)

    def cost_step(index, carry):
        k, side = index // 2, lax.rem(index, 2)
        h = h_me + (2 * side - 1) * k

        @pl.when(jnp.logical_and(jnp.logical_and(h >= 0, h < halves_t), k + side > 0))
        def _():
            cost_rows(h)

        @pl.when(index == 1)
        def _():
            for k in range(3, halves_t):
                forward(k)

        return carry

    lax.fori_loop(1, 2 * halves_t, cost_step, 0)
    if pair % LANES != 0:
        for c in range(row_chunks):
            first_row_sums(c)
    x_rp[0]()
    x_rp[1]()

    def merge(buf, n, chunks):
        best = buf[0, :chunks, :]
        for d in range(1, n):
            best = jnp.maximum(best, buf[d, :chunks, :])
        total = jnp.zeros_like(best)
        for d in range(n):
            total += buf[d, chunks:, :] * jnp.exp2(buf[d, :chunks, :] - best)
        return best + jnp.log(total) * LOG2E

    def to_col(packed):
        for c in range(row_chunks):
            col[rows_of(c), :] = jnp.broadcast_to(packed[c:c + 1, :], (LANES, LANES)).T

    f_pot = -(math.log2(src_total) + merge(row_pair, n_t, row_chunks))
    to_col(f_pot)

    tops = []
    for k in range(col_chunks):
        def top_step(c, best, k=k):
            rows = pl.ds(pl.multiple_of(c * LANES, LANES), LANES)
            z = col[rows, :] - tile[rows, rows_of(k)]
            return jnp.maximum(best, jnp.max(z.reshape(LANES // 8, 8, LANES), axis=0))

        best = lax.fori_loop(0, row_chunks, top_step, jnp.full((8, LANES), -jnp.inf, f32), unroll=True)
        best = jnp.max(best, axis=0, keepdims=True)
        tops.append(best)

        def exp_step(c, total, k=k, best=best):
            rows = pl.ds(pl.multiple_of(c * LANES, LANES), LANES)
            e = jnp.exp2(col[rows, :] - tile[rows, rows_of(k)] - best)
            tile[rows, rows_of(k)] = e
            return total + jnp.sum(e.reshape(LANES // 8, 8, LANES), axis=0)

        total = lax.fori_loop(0, row_chunks, exp_step, jnp.zeros((8, LANES), f32), unroll=True)
        col_pair[s_me, k:k + 1, :] = best
        col_pair[s_me, col_chunks + k:col_chunks + k + 1, :] = jnp.sum(total, axis=0, keepdims=True)
    x_cp[0]()
    x_cp[1]()
    g_first = -(math.log2(tgt_total) + merge(col_pair, n_s, col_chunks))
    base = jnp.exp2(jnp.concatenate(tops, axis=0) + g_first)
    b = base

    def row_products(slot, b):
        for c in range(row_chunks):
            total = tile[rows_of(c), rows_of(0)] * b[0:1, :]
            for k in range(1, col_chunks):
                total += tile[rows_of(c), rows_of(k)] * b[k:k + 1, :]
            row_sum[slot, t_me, c:c + 1, :] = jnp.sum(total.T, axis=0, keepdims=True)

    def add_up(buf, slot, n):
        total = buf[slot, 0]
        for d in range(1, n):
            total += buf[slot, d]
        return total

    for it in range(ITERS - 1):
        row_products(it, b)
        x_rs[it][0]()
        x_rs[it][1]()
        to_col(1.0 / (src_total * add_up(row_sum, it, n_t)))
        for k in range(col_chunks):
            total = jnp.zeros((8, LANES), f32)
            for c in range(row_chunks):
                e = tile[rows_of(c), rows_of(k)] * col[rows_of(c), :]
                total += jnp.sum(e.reshape(LANES // 8, 8, LANES), axis=0)
            col_sum[it, s_me, k:k + 1, :] = jnp.sum(total, axis=0, keepdims=True) * base[k:k + 1, :]
        x_cs[it][0]()
        x_cs[it][1]()
        beta = 1.0 / (tgt_total * add_up(col_sum, it, n_s))
        b = base * beta
    pot_ref[...] = EPS * (g_first * math.log(2.0) + jnp.log(beta))

    last = ITERS - 1
    row_products(last, b)
    x_rs[last][0]()
    for k in range(col_chunks):
        t_hi, t_lo = split(tgt_all[:, rows_of(k)] * b[k:k + 1, :])
        tgt_hi[:, rows_of(k)] = t_hi
        tgt_lo[:, rows_of(k)] = t_lo

    dims = (((1,), (1,)), ((), ()))

    def send_x(h, lo):
        return pltpu.make_async_remote_copy(
            src_ref=bary.at[pl.ds(pl.multiple_of((h * 2 + lo) * rows_own, 8), rows_own), :], dst_ref=from_x.at[h],
            send_sem=ax_s.at[h], recv_sem=ax_r.at[h], device_id=on_tgt(h_me * 2 + 1 - l_me), device_id_type=MESH)

    def send_z(h, sender):
        return pltpu.make_async_remote_copy(
            src_ref=to_z.at[h], dst_ref=from_z.at[sender], send_sem=bz_s.at[h], recv_sem=bz_r.at[sender],
            device_id=on_tgt(h * 2 + l_me), device_id_type=MESH)

    def own_rows(h):
        return bary[pl.ds(pl.multiple_of((h * 2 + l_me) * rows_own, 8), rows_own), :]

    def compute(h):
        rows = pl.ds(pl.multiple_of(h * pair, 16), pair)
        e_hi, e_lo = split(tile[rows, :])
        out = lax.dot_general(e_hi, tgt_hi[...], dims, preferred_element_type=f32)
        out += lax.dot_general(e_hi, tgt_lo[...], dims, preferred_element_type=f32)
        out += lax.dot_general(e_lo, tgt_hi[...], dims, preferred_element_type=f32)
        bary[rows, :] = out
        send_x(h, 1 - l_me).start()

    def pass_on(h):
        send_x(h, 1 - l_me).wait_recv()
        to_z[h] = own_rows(h) + from_x[h]
        send_z(h, h_me).start()

    def step(off, carry):
        compute(lax.rem(h_me + off, halves_t))

        @pl.when(off > 1)
        def _():
            pass_on(lax.rem(h_me + off - 1, halves_t))

        return carry

    lax.fori_loop(1, halves_t + 1, step, 0)
    x_rs[last][1]()
    to_col(1.0 / add_up(row_sum, last, n_t))
    send_x(h_me, 1 - l_me).wait_recv()
    total = own_rows(h_me) + from_x[h_me]
    for off in range(1, halves_t):
        h = lax.rem(h_me + off, halves_t)
        send_z(h, h).wait_recv()
        total += from_z[h]
    inv = col[pl.ds(pl.multiple_of(t_me * rows_own, 8), rows_own), :]
    inv = jnp.concatenate([inv] * (feat // LANES), axis=1)
    vel_ref[...] = total * inv - noise_ref[...]

    drain_src()
    g_tgt[3]()
    for ops in [x_rp, x_cp] + x_rs + x_cs:
        ops[2]()
    for off in range(1, halves_t):
        h = lax.rem(h_me + off, halves_t)
        send_x(h, 1 - l_me).wait_send()
        send_z(h, h_me).wait_send()
    send_x(h_me, 1 - l_me).wait_send()


def per_device(n_s, n_t, noise, data):
    rows_own, feat = noise.shape
    n_rows, n_cols = rows_own * n_t, data.shape[0]
    rc, cc = n_rows // LANES, n_cols // LANES
    nh, nhs = n_t // 2, n_s // 2
    f32, bf16 = jnp.float32, jnp.bfloat16
    vmem = pltpu.VMEM
    dma = pltpu.SemaphoreType.DMA
    vel, pot = pl.pallas_call(
        functools.partial(kernel, n_s, n_t),
        out_shape=(jax.ShapeDtypeStruct((rows_own, feat), f32), jax.ShapeDtypeStruct((cc, LANES), f32)),
        in_specs=[pl.BlockSpec(memory_space=vmem)] * 2,
        out_specs=(pl.BlockSpec(memory_space=vmem), pl.BlockSpec(memory_space=vmem)),
        scratch_shapes=[
            vmem((n_rows, feat), f32), vmem((feat, n_cols), f32),
            vmem((feat, n_cols), bf16), vmem((feat, n_cols), bf16),
            vmem((n_rows, n_cols), f32), vmem((n_rows, LANES), f32), vmem((n_rows, feat), f32),
            vmem((n_t, 2 * rc, LANES), f32), vmem((n_s, 2 * cc, LANES), f32),
            vmem((ITERS, n_t, rc, LANES), f32), vmem((ITERS - 1, n_s, cc, LANES), f32),
            vmem((nh, rows_own, feat), f32), vmem((nh, rows_own, feat), f32), vmem((nh, rows_own, feat), f32),
            dma((nh,)), dma((nh,)), dma((nh,)), dma((nh,)), dma((nh,)),
            dma((nhs,)), dma((nhs,)), dma((nhs,)), dma((nhs,)),
            dma((n_t,)), dma((n_t,)), dma((n_s,)), dma((n_s,)),
            dma((ITERS, n_t)), dma((ITERS, n_t)), dma((ITERS - 1, n_s)), dma((ITERS - 1, n_s)),
            dma((nh,)), dma((nh,)), dma((nh,)), dma((nh,)),
        ],
        compiler_params=pltpu.CompilerParams(
            collective_id=0, has_side_effects=True, vmem_limit_bytes=48 * 1024 * 1024),
    )(noise, data)
    return vel, pot.reshape(n_cols)


def solution(mesh):
    return jax.shard_map(
        functools.partial(per_device, mesh.shape["src"], mesh.shape["tgt"]),
        mesh=mesh,
        in_specs=(P(("src", "tgt"), None), P("tgt", "src")),
        out_specs=(P(("src", "tgt"), None), P("tgt")),
        check_vma=False,
    )
```

```python
import functools
import math

import jax
import jax.numpy as jnp
from jax import lax
from jax.experimental import pallas as pl
from jax.experimental.pallas import tpu as pltpu
from jax.sharding import PartitionSpec as P

ITERS = 3
EPS = 0.05
LOG2E = 1.0 / math.log(2.0)
LANES = 128
MESH = pl.DeviceIdType.MESH


def split(value):
    high = value.astype(jnp.bfloat16)
    return high, (value - high.astype(jnp.float32)).astype(jnp.bfloat16)


def kernel(n_s, n_t, noise_ref, data_ref, vel_ref, pot_ref, src_all, tgt_all, tgt_hi, tgt_lo, tile, col, bary,
           row_pair, col_pair, row_sum, col_sum, from_x, to_z, from_z,
           src_us, src_ds, src_rs, src_fs, src_fr, tgt_ss, tgt_rs, tgt_fs, tgt_fr,
           rp_s, rp_r, cp_s, cp_r, rs_s, rs_r, cs_s, cs_r, ax_s, ax_r, bz_s, bz_r):
    s_me, t_me = lax.axis_index("src"), lax.axis_index("tgt")
    rows_own, feat = noise_ref.shape
    feat_own = data_ref.shape[0]
    n_rows, n_cols = tile.shape
    row_chunks, col_chunks = n_rows // LANES, n_cols // LANES
    src_total, tgt_total = n_rows * n_s, n_cols * n_t
    halves_t = n_t // 2
    f32 = jnp.float32

    def on_tgt(peer):
        return (s_me, peer)

    def on_src(peer):
        return (peer, t_me)

    barrier = pltpu.get_barrier_semaphore()
    for off in range(1, n_t):
        pl.semaphore_signal(barrier, 1, device_id=on_tgt(lax.rem(t_me + off, n_t)), device_id_type=MESH)
    for off in range(1, n_s):
        pl.semaphore_signal(barrier, 1, device_id=on_src(lax.rem(s_me + off, n_s)), device_id_type=MESH)
    tgt_all[pl.ds(pl.multiple_of(s_me * feat_own, 8), feat_own), :] = data_ref[...]
    src_all[pl.ds(pl.multiple_of(t_me * rows_own, 8), rows_own), :] = noise_ref[...]
    pl.semaphore_wait(barrier, n_t + n_s - 2)

    def gather_ops(buf, rows, n, me, dev_of, ss, rs, fs, fr):
        hi, lo = me // 2, lax.rem(me, 2)
        nh = n // 2

        def block(idx):
            return buf.at[pl.ds(pl.multiple_of(idx * rows, 8), rows), :]

        def far(h, owner):
            return pltpu.make_async_remote_copy(
                src_ref=block(owner), dst_ref=block(owner), send_sem=ss.at[h], recv_sem=rs.at[owner // 2],
                device_id=dev_of(h * 2 + lo), device_id_type=MESH)

        def near(owner, h):
            return pltpu.make_async_remote_copy(
                src_ref=block(owner), dst_ref=block(owner), send_sem=fs.at[h], recv_sem=fr.at[h],
                device_id=dev_of(hi * 2 + 1 - lo), device_id_type=MESH)

        offs = list(range(1, nh))

        def begin():
            for off in offs:
                far(lax.rem(hi + off, nh), me).start()
            near(me, hi).start()

        def forward():
            for off in offs:
                h = lax.rem(hi + off, nh)
                far(h, h * 2 + lo).wait_recv()
                near(h * 2 + lo, h).start()

        def finish():
            for off in [0] + offs:
                h = lax.rem(hi + off, nh)
                near(h * 2 + 1 - lo, h).wait_recv()

        def drain():
            for off in offs:
                far(lax.rem(hi + off, nh), me).wait_send()
            for off in [0] + offs:
                h = lax.rem(hi + off, nh)
                near(h * 2 + lo, h).wait_send()

        return begin, forward, finish, drain

    h_me, l_me = t_me // 2, lax.rem(t_me, 2)
    partner = h_me * 2 + 1 - l_me

    def src_copy(h, low, send, recv, dev):
        ref = src_all.at[pl.ds(pl.multiple_of((h * 2 + low) * rows_own, 8), rows_own), :]
        return pltpu.make_async_remote_copy(
            src_ref=ref, dst_ref=ref, send_sem=send.at[h], recv_sem=recv.at[h],
            device_id=on_tgt(dev), device_id_type=MESH)

    def up(h):
        return src_copy(h, l_me, src_us, src_rs, t_me + 2)

    def down(h):
        return src_copy(h, l_me, src_ds, src_rs, t_me - 2)

    def near(h):
        return src_copy(h, l_me, src_fs, src_fr, partner)

    def send_on(h, go_up, go_down):
        if go_up:
            @pl.when(h_me < halves_t - 1)
            def _():
                up(h).start()
        if go_down:
            @pl.when(h_me > 0)
            def _():
                down(h).start()
        near(h).start()

    def forward(k):
        @pl.when(h_me - k >= 0)
        def _():
            src_copy(h_me - k, l_me, src_us, src_rs, partner).wait_recv()
            send_on(h_me - k, True, False)

        @pl.when(h_me + k < halves_t)
        def _():
            src_copy(h_me + k, l_me, src_ds, src_rs, partner).wait_recv()
            send_on(h_me + k, False, True)

    def drain_src():
        for h in range(halves_t):
            @pl.when(jnp.logical_and(h <= h_me, h_me < halves_t - 1))
            def _(h=h):
                up(h).wait_send()

            @pl.when(jnp.logical_and(h >= h_me, h_me > 0))
            def _(h=h):
                down(h).wait_send()

            near(h).wait_send()

    g_tgt = gather_ops(tgt_all, feat_own, n_s, s_me, on_src, tgt_ss, tgt_rs, tgt_fs, tgt_fr)
    send_on(h_me, True, True)
    g_tgt[0]()
    forward(1)
    g_tgt[1]()
    forward(2)
    g_tgt[2]()

    def exchange(buf, n, me, dev_of, ss, rs):
        def op(peer, owner):
            return pltpu.make_async_remote_copy(
                src_ref=buf.at[owner], dst_ref=buf.at[owner], send_sem=ss.at[peer], recv_sem=rs.at[owner],
                device_id=dev_of(peer), device_id_type=MESH)

        def start():
            for off in range(1, n):
                op(lax.rem(me + off, n), me).start()

        def wait():
            for off in range(1, n):
                peer = lax.rem(me + off, n)
                op(peer, peer).wait_recv()

        def drain():
            for off in range(1, n):
                op(lax.rem(me + off, n), me).wait_send()

        return start, wait, drain

    x_rp = exchange(row_pair, n_t, t_me, on_tgt, rp_s, rp_r)
    x_cp = exchange(col_pair, n_s, s_me, on_src, cp_s, cp_r)
    x_rs = [exchange(row_sum.at[k], n_t, t_me, on_tgt, rs_s.at[k], rs_r.at[k]) for k in range(ITERS)]
    x_cs = [exchange(col_sum.at[k], n_s, s_me, on_src, cs_s.at[k], cs_r.at[k]) for k in range(ITERS - 1)]

    scale = LOG2E / (feat * EPS)
    t_hi, t_lo = split(tgt_all[...])
    tgt_hi[...] = t_hi
    tgt_lo[...] = t_lo
    target_sq = jnp.sum(tgt_all[...] * tgt_all[...], axis=0, keepdims=True)
    pair = 2 * rows_own

    def rows_of(c):
        return slice(c * LANES, (c + 1) * LANES)

    def first_row_sums(c):
        rows = pl.ds(pl.multiple_of(c * LANES, LANES), LANES)
        top = -tile[rows, rows_of(0)]
        for k in range(1, col_chunks):
            top = jnp.maximum(top, -tile[rows, rows_of(k)])
        total = jnp.zeros_like(top)
        for k in range(col_chunks):
            total += jnp.exp2(-tile[rows, rows_of(k)] - top)
        top, total = top.T, total.T
        best = jnp.max(top, axis=0, keepdims=True)
        row_pair[t_me, pl.ds(c, 1), :] = best
        row_pair[t_me, pl.ds(row_chunks + c, 1), :] = jnp.sum(total * jnp.exp2(top - best), axis=0, keepdims=True)

    def cost_rows(h):
        src_copy(h, 1 - l_me, src_fs, src_fr, partner).wait_recv()
        rows = pl.ds(pl.multiple_of(h * pair, 16), pair)
        source = src_all[rows, :]
        source_sq = jnp.sum(source * source, axis=1, keepdims=True)
        s_hi, s_lo = split(source)
        cross = jnp.dot(s_hi, tgt_hi[...], preferred_element_type=f32)
        cross += jnp.dot(s_hi, tgt_lo[...], preferred_element_type=f32)
        cross += jnp.dot(s_lo, tgt_hi[...], preferred_element_type=f32)
        tile[rows, :] = (source_sq + target_sq - 2.0 * cross) * scale
        if pair % LANES == 0:
            for c in range(pair // LANES):
                first_row_sums(h * (pair // LANES) + c)

    def cost_step(index, carry):
        k, side = index // 2, lax.rem(index, 2)
        h = h_me + (2 * side - 1) * k

        @pl.when(jnp.logical_and(jnp.logical_and(h >= 0, h < halves_t), k + side > 0))
        def _():
            cost_rows(h)

        @pl.when(index == 1)
        def _():
            for k in range(3, halves_t):
                forward(k)

        return carry

    lax.fori_loop(1, 2 * halves_t, cost_step, 0)
    if pair % LANES != 0:
        for c in range(row_chunks):
            first_row_sums(c)
    x_rp[0]()
    x_rp[1]()

    def merge(buf, n, chunks):
        best = buf[0, :chunks, :]
        for d in range(1, n):
            best = jnp.maximum(best, buf[d, :chunks, :])
        total = jnp.zeros_like(best)
        for d in range(n):
            total += buf[d, chunks:, :] * jnp.exp2(buf[d, :chunks, :] - best)
        return best + jnp.log(total) * LOG2E

    def to_col(packed):
        for c in range(row_chunks):
            col[rows_of(c), :] = jnp.broadcast_to(packed[c:c + 1, :], (LANES, LANES)).T

    f_pot = -(math.log2(src_total) + merge(row_pair, n_t, row_chunks))
    to_col(f_pot)

    tops = []
    for k in range(col_chunks):
        def top_step(c, best, k=k):
            rows = pl.ds(pl.multiple_of(c * LANES, LANES), LANES)
            z = col[rows, :] - tile[rows, rows_of(k)]
            return jnp.maximum(best, jnp.max(z.reshape(LANES // 8, 8, LANES), axis=0))

        best = lax.fori_loop(0, row_chunks, top_step, jnp.full((8, LANES), -jnp.inf, f32), unroll=True)
        best = jnp.max(best, axis=0, keepdims=True)
        tops.append(best)

        def exp_step(c, total, k=k, best=best):
            rows = pl.ds(pl.multiple_of(c * LANES, LANES), LANES)
            e = jnp.exp2(col[rows, :] - tile[rows, rows_of(k)] - best)
            tile[rows, rows_of(k)] = e
            return total + jnp.sum(e.reshape(LANES // 8, 8, LANES), axis=0)

        total = lax.fori_loop(0, row_chunks, exp_step, jnp.zeros((8, LANES), f32), unroll=True)
        col_pair[s_me, k:k + 1, :] = best
        col_pair[s_me, col_chunks + k:col_chunks + k + 1, :] = jnp.sum(total, axis=0, keepdims=True)
    x_cp[0]()
    x_cp[1]()
    g_first = -(math.log2(tgt_total) + merge(col_pair, n_s, col_chunks))
    base = jnp.exp2(jnp.concatenate(tops, axis=0) + g_first)
    b = base

    def row_products(slot, b):
        for c in range(row_chunks):
            total = tile[rows_of(c), rows_of(0)] * b[0:1, :]
            for k in range(1, col_chunks):
                total += tile[rows_of(c), rows_of(k)] * b[k:k + 1, :]
            row_sum[slot, t_me, c:c + 1, :] = jnp.sum(total.T, axis=0, keepdims=True)

    def add_up(buf, slot, n):
        total = buf[slot, 0]
        for d in range(1, n):
            total += buf[slot, d]
        return total

    for it in range(ITERS - 1):
        row_products(it, b)
        x_rs[it][0]()
        x_rs[it][1]()
        to_col(1.0 / (src_total * add_up(row_sum, it, n_t)))
        for k in range(col_chunks):
            total = jnp.zeros((8, LANES), f32)
            for c in range(row_chunks):
                e = tile[rows_of(c), rows_of(k)] * col[rows_of(c), :]
                total += jnp.sum(e.reshape(LANES // 8, 8, LANES), axis=0)
            col_sum[it, s_me, k:k + 1, :] = jnp.sum(total, axis=0, keepdims=True) * base[k:k + 1, :]
        x_cs[it][0]()
        x_cs[it][1]()
        beta = 1.0 / (tgt_total * add_up(col_sum, it, n_s))
        b = base * beta
    pot_ref[...] = EPS * (g_first * math.log(2.0) + jnp.log(beta))

    last = ITERS - 1
    for k in range(col_chunks):
        t_hi, t_lo = split(tgt_all[:, rows_of(k)] * b[k:k + 1, :])
        tgt_hi[:, rows_of(k)] = t_hi
        tgt_lo[:, rows_of(k)] = t_lo

    dims = (((1,), (1,)), ((), ()))

    def send_x(h, lo):
        return pltpu.make_async_remote_copy(
            src_ref=bary.at[pl.ds(pl.multiple_of((h * 2 + lo) * rows_own, 8), rows_own), :], dst_ref=from_x.at[h],
            send_sem=ax_s.at[h], recv_sem=ax_r.at[h], device_id=on_tgt(h_me * 2 + 1 - l_me), device_id_type=MESH)

    def send_z(h, sender):
        return pltpu.make_async_remote_copy(
            src_ref=to_z.at[h], dst_ref=from_z.at[sender], send_sem=bz_s.at[h], recv_sem=bz_r.at[sender],
            device_id=on_tgt(h * 2 + l_me), device_id_type=MESH)

    def own_rows(h):
        return bary[pl.ds(pl.multiple_of((h * 2 + l_me) * rows_own, 8), rows_own), :]

    def compute(h):
        product(h, 1 - l_me)
        send_x(h, 1 - l_me).start()
        product(h, l_me)

    def product(h, lo):
        rows = pl.ds(pl.multiple_of((h * 2 + lo) * rows_own, 16), rows_own)
        e_hi, e_lo = split(tile[rows, :])
        out = lax.dot_general(e_hi, tgt_hi[...], dims, preferred_element_type=f32)
        out += lax.dot_general(e_hi, tgt_lo[...], dims, preferred_element_type=f32)
        out += lax.dot_general(e_lo, tgt_hi[...], dims, preferred_element_type=f32)
        bary[rows, :] = out

    def pass_on(h):
        send_x(h, 1 - l_me).wait_recv()
        to_z[h] = own_rows(h) + from_x[h]
        send_z(h, h_me).start()

    def step(off, carry):
        compute(lax.rem(h_me + off, halves_t))

        @pl.when(off == 1)
        def _():
            row_products(last, b)
            x_rs[last][0]()

        @pl.when(off > 1)
        def _():
            pass_on(lax.rem(h_me + off - 1, halves_t))

        return carry

    lax.fori_loop(1, halves_t + 1, step, 0)
    x_rs[last][1]()
    to_col(1.0 / add_up(row_sum, last, n_t))
    send_x(h_me, 1 - l_me).wait_recv()
    total = own_rows(h_me) + from_x[h_me]
    for off in range(1, halves_t):
        h = lax.rem(h_me + off, halves_t)
        send_z(h, h).wait_recv()
        total += from_z[h]
    inv = col[pl.ds(pl.multiple_of(t_me * rows_own, 8), rows_own), :]
    inv = jnp.concatenate([inv] * (feat // LANES), axis=1)
    vel_ref[...] = total * inv - noise_ref[...]

    drain_src()
    g_tgt[3]()
    for ops in [x_rp, x_cp] + x_rs + x_cs:
        ops[2]()
    for off in range(1, halves_t):
        h = lax.rem(h_me + off, halves_t)
        send_x(h, 1 - l_me).wait_send()
        send_z(h, h_me).wait_send()
    send_x(h_me, 1 - l_me).wait_send()


def per_device(n_s, n_t, noise, data):
    rows_own, feat = noise.shape
    n_rows, n_cols = rows_own * n_t, data.shape[0]
    rc, cc = n_rows // LANES, n_cols // LANES
    nh, nhs = n_t // 2, n_s // 2
    f32, bf16 = jnp.float32, jnp.bfloat16
    vmem = pltpu.VMEM
    dma = pltpu.SemaphoreType.DMA
    vel, pot = pl.pallas_call(
        functools.partial(kernel, n_s, n_t),
        out_shape=(jax.ShapeDtypeStruct((rows_own, feat), f32), jax.ShapeDtypeStruct((cc, LANES), f32)),
        in_specs=[pl.BlockSpec(memory_space=vmem)] * 2,
        out_specs=(pl.BlockSpec(memory_space=vmem), pl.BlockSpec(memory_space=vmem)),
        scratch_shapes=[
            vmem((n_rows, feat), f32), vmem((feat, n_cols), f32),
            vmem((feat, n_cols), bf16), vmem((feat, n_cols), bf16),
            vmem((n_rows, n_cols), f32), vmem((n_rows, LANES), f32), vmem((n_rows, feat), f32),
            vmem((n_t, 2 * rc, LANES), f32), vmem((n_s, 2 * cc, LANES), f32),
            vmem((ITERS, n_t, rc, LANES), f32), vmem((ITERS - 1, n_s, cc, LANES), f32),
            vmem((nh, rows_own, feat), f32), vmem((nh, rows_own, feat), f32), vmem((nh, rows_own, feat), f32),
            dma((nh,)), dma((nh,)), dma((nh,)), dma((nh,)), dma((nh,)),
            dma((nhs,)), dma((nhs,)), dma((nhs,)), dma((nhs,)),
            dma((n_t,)), dma((n_t,)), dma((n_s,)), dma((n_s,)),
            dma((ITERS, n_t)), dma((ITERS, n_t)), dma((ITERS - 1, n_s)), dma((ITERS - 1, n_s)),
            dma((nh,)), dma((nh,)), dma((nh,)), dma((nh,)),
        ],
        compiler_params=pltpu.CompilerParams(
            collective_id=0, has_side_effects=True, vmem_limit_bytes=48 * 1024 * 1024),
    )(noise, data.T)
    return vel, pot.reshape(n_cols)


def solution(mesh):
    return jax.shard_map(
        functools.partial(per_device, mesh.shape["src"], mesh.shape["tgt"]),
        mesh=mesh,
        in_specs=(P(("src", "tgt"), None), P("tgt", "src")),
        out_specs=(P(("src", "tgt"), None), P("tgt")),
        check_vma=False,
    )
```

```python
import functools
import math

import jax
import jax.numpy as jnp
from jax import lax
from jax.experimental import pallas as pl
from jax.experimental.pallas import tpu as pltpu
from jax.sharding import PartitionSpec as P

ITERS = 3
EPS = 0.05
LOG2E = 1.0 / math.log(2.0)
LANES = 128
MESH = pl.DeviceIdType.MESH


def split(value):
    high = value.astype(jnp.bfloat16)
    return high, (value - high.astype(jnp.float32)).astype(jnp.bfloat16)


def kernel(n_s, n_t, noise_ref, data_ref, vel_ref, pot_ref, src_all, tgt_all, tgt_hi, tgt_lo, tile, col, bary,
           row_pair, col_pair, row_sum, col_sum, from_x, to_z, from_z,
           src_us, src_ds, src_rs, src_fs, src_fr, tgt_ss, tgt_rs, tgt_fs, tgt_fr,
           rp_s, rp_r, cp_s, cp_r, rs_s, rs_r, cs_s, cs_r, ax_s, ax_r, bz_s, bz_r):
    s_me, t_me = lax.axis_index("src"), lax.axis_index("tgt")
    rows_own, feat = noise_ref.shape
    feat_own = data_ref.shape[0]
    n_rows, n_cols = tile.shape
    row_chunks, col_chunks = n_rows // LANES, n_cols // LANES
    src_total, tgt_total = n_rows * n_s, n_cols * n_t
    halves_t = n_t // 2
    f32 = jnp.float32

    def on_tgt(peer):
        return (s_me, peer)

    def on_src(peer):
        return (peer, t_me)

    barrier = pltpu.get_barrier_semaphore()
    for off in range(1, n_t):
        pl.semaphore_signal(barrier, 1, device_id=on_tgt(lax.rem(t_me + off, n_t)), device_id_type=MESH)
    for off in range(1, n_s):
        pl.semaphore_signal(barrier, 1, device_id=on_src(lax.rem(s_me + off, n_s)), device_id_type=MESH)
    tgt_all[pl.ds(pl.multiple_of(s_me * feat_own, 8), feat_own), :] = data_ref[...]
    src_all[pl.ds(pl.multiple_of(t_me * rows_own, 8), rows_own), :] = noise_ref[...]
    pl.semaphore_wait(barrier, n_t + n_s - 2)

    def gather_ops(buf, rows, n, me, dev_of, ss, rs, fs, fr):
        hi, lo = me // 2, lax.rem(me, 2)
        nh = n // 2

        def block(idx):
            return buf.at[pl.ds(pl.multiple_of(idx * rows, 8), rows), :]

        def far(h, owner):
            return pltpu.make_async_remote_copy(
                src_ref=block(owner), dst_ref=block(owner), send_sem=ss.at[h], recv_sem=rs.at[owner // 2],
                device_id=dev_of(h * 2 + lo), device_id_type=MESH)

        def near(owner, h):
            return pltpu.make_async_remote_copy(
                src_ref=block(owner), dst_ref=block(owner), send_sem=fs.at[h], recv_sem=fr.at[h],
                device_id=dev_of(hi * 2 + 1 - lo), device_id_type=MESH)

        offs = list(range(1, nh))

        def begin():
            for off in offs:
                far(lax.rem(hi + off, nh), me).start()
            near(me, hi).start()

        def forward():
            for off in offs:
                h = lax.rem(hi + off, nh)
                far(h, h * 2 + lo).wait_recv()
                near(h * 2 + lo, h).start()

        def finish():
            for off in [0] + offs:
                h = lax.rem(hi + off, nh)
                near(h * 2 + 1 - lo, h).wait_recv()

        def drain():
            for off in offs:
                far(lax.rem(hi + off, nh), me).wait_send()
            for off in [0] + offs:
                h = lax.rem(hi + off, nh)
                near(h * 2 + lo, h).wait_send()

        return begin, forward, finish, drain

    h_me, l_me = t_me // 2, lax.rem(t_me, 2)
    partner = h_me * 2 + 1 - l_me

    def src_copy(h, low, send, recv, dev):
        ref = src_all.at[pl.ds(pl.multiple_of((h * 2 + low) * rows_own, 8), rows_own), :]
        return pltpu.make_async_remote_copy(
            src_ref=ref, dst_ref=ref, send_sem=send.at[h], recv_sem=recv.at[h],
            device_id=on_tgt(dev), device_id_type=MESH)

    def up(h):
        return src_copy(h, l_me, src_us, src_rs, t_me + 2)

    def down(h):
        return src_copy(h, l_me, src_ds, src_rs, t_me - 2)

    def near(h):
        return src_copy(h, l_me, src_fs, src_fr, partner)

    def send_on(h, go_up, go_down):
        if go_up:
            @pl.when(h_me < halves_t - 1)
            def _():
                up(h).start()
        if go_down:
            @pl.when(h_me > 0)
            def _():
                down(h).start()
        near(h).start()

    def forward(k):
        @pl.when(h_me - k >= 0)
        def _():
            src_copy(h_me - k, l_me, src_us, src_rs, partner).wait_recv()
            send_on(h_me - k, True, False)

        @pl.when(h_me + k < halves_t)
        def _():
            src_copy(h_me + k, l_me, src_ds, src_rs, partner).wait_recv()
            send_on(h_me + k, False, True)

    def drain_src():
        for h in range(halves_t):
            @pl.when(jnp.logical_and(h <= h_me, h_me < halves_t - 1))
            def _(h=h):
                up(h).wait_send()

            @pl.when(jnp.logical_and(h >= h_me, h_me > 0))
            def _(h=h):
                down(h).wait_send()

            near(h).wait_send()

    g_tgt = gather_ops(tgt_all, feat_own, n_s, s_me, on_src, tgt_ss, tgt_rs, tgt_fs, tgt_fr)
    send_on(h_me, True, True)
    g_tgt[0]()
    forward(1)
    g_tgt[1]()
    forward(2)
    g_tgt[2]()

    def exchange(buf, n, me, dev_of, ss, rs):
        def op(peer, owner):
            return pltpu.make_async_remote_copy(
                src_ref=buf.at[owner], dst_ref=buf.at[owner], send_sem=ss.at[peer], recv_sem=rs.at[owner],
                device_id=dev_of(peer), device_id_type=MESH)

        def start():
            for off in range(1, n):
                op(lax.rem(me + off, n), me).start()

        def wait():
            for off in range(1, n):
                peer = lax.rem(me + off, n)
                op(peer, peer).wait_recv()

        def drain():
            for off in range(1, n):
                op(lax.rem(me + off, n), me).wait_send()

        return start, wait, drain

    x_rp = exchange(row_pair, n_t, t_me, on_tgt, rp_s, rp_r)
    x_cp = exchange(col_pair, n_s, s_me, on_src, cp_s, cp_r)
    x_rs = [exchange(row_sum.at[k], n_t, t_me, on_tgt, rs_s.at[k], rs_r.at[k]) for k in range(ITERS)]
    x_cs = [exchange(col_sum.at[k], n_s, s_me, on_src, cs_s.at[k], cs_r.at[k]) for k in range(ITERS - 1)]

    scale = LOG2E / (feat * EPS)
    t_hi, t_lo = split(tgt_all[...])
    tgt_hi[...] = t_hi
    tgt_lo[...] = t_lo
    target_sq = jnp.sum(tgt_all[...] * tgt_all[...], axis=0, keepdims=True)
    pair = 2 * rows_own

    def rows_of(c):
        return slice(c * LANES, (c + 1) * LANES)

    def first_row_sums(c):
        rows = pl.ds(pl.multiple_of(c * LANES, LANES), LANES)
        top = -tile[rows, rows_of(0)]
        for k in range(1, col_chunks):
            top = jnp.maximum(top, -tile[rows, rows_of(k)])
        total = jnp.zeros_like(top)
        for k in range(col_chunks):
            total += jnp.exp2(-tile[rows, rows_of(k)] - top)
        top, total = top.T, total.T
        best = jnp.max(top, axis=0, keepdims=True)
        row_pair[t_me, pl.ds(c, 1), :] = best
        row_pair[t_me, pl.ds(row_chunks + c, 1), :] = jnp.sum(total * jnp.exp2(top - best), axis=0, keepdims=True)

    def cost_rows(h):
        src_copy(h, 1 - l_me, src_fs, src_fr, partner).wait_recv()
        rows = pl.ds(pl.multiple_of(h * pair, 16), pair)
        source = src_all[rows, :]
        source_sq = jnp.sum(source * source, axis=1, keepdims=True)
        s_hi, s_lo = split(source)
        cross = jnp.dot(s_hi, tgt_hi[...], preferred_element_type=f32)
        cross += jnp.dot(s_hi, tgt_lo[...], preferred_element_type=f32)
        cross += jnp.dot(s_lo, tgt_hi[...], preferred_element_type=f32)
        tile[rows, :] = (source_sq + target_sq - 2.0 * cross) * scale
        if pair % LANES == 0:
            for c in range(pair // LANES):
                first_row_sums(h * (pair // LANES) + c)

    def cost_step(index, carry):
        k, side = index // 2, lax.rem(index, 2)
        h = h_me + (2 * side - 1) * k

        @pl.when(jnp.logical_and(jnp.logical_and(h >= 0, h < halves_t), k + side > 0))
        def _():
            cost_rows(h)

        @pl.when(index == 1)
        def _():
            for k in range(3, halves_t):
                forward(k)

        return carry

    lax.fori_loop(1, 2 * halves_t, cost_step, 0)
    if pair % LANES != 0:
        for c in range(row_chunks):
            first_row_sums(c)
    x_rp[0]()
    x_rp[1]()

    def merge(buf, n, chunks):
        best = buf[0, :chunks, :]
        for d in range(1, n):
            best = jnp.maximum(best, buf[d, :chunks, :])
        total = jnp.zeros_like(best)
        for d in range(n):
            total += buf[d, chunks:, :] * jnp.exp2(buf[d, :chunks, :] - best)
        return best + jnp.log(total) * LOG2E

    def to_col(packed):
        for c in range(row_chunks):
            col[rows_of(c), :] = jnp.broadcast_to(packed[c:c + 1, :], (LANES, LANES)).T

    f_pot = -(math.log2(src_total) + merge(row_pair, n_t, row_chunks))
    to_col(f_pot)

    tops = []
    for k in range(col_chunks):
        def top_step(c, best, k=k):
            rows = pl.ds(pl.multiple_of(c * LANES, LANES), LANES)
            z = col[rows, :] - tile[rows, rows_of(k)]
            return jnp.maximum(best, jnp.max(z.reshape(LANES // 8, 8, LANES), axis=0))

        best = lax.fori_loop(0, row_chunks, top_step, jnp.full((8, LANES), -jnp.inf, f32), unroll=True)
        best = jnp.max(best, axis=0, keepdims=True)
        tops.append(best)

        def exp_step(c, total, k=k, best=best):
            rows = pl.ds(pl.multiple_of(c * LANES, LANES), LANES)
            e = jnp.exp2(col[rows, :] - tile[rows, rows_of(k)] - best)
            tile[rows, rows_of(k)] = e
            return total + jnp.sum(e.reshape(LANES // 8, 8, LANES), axis=0)

        total = lax.fori_loop(0, row_chunks, exp_step, jnp.zeros((8, LANES), f32), unroll=True)
        col_pair[s_me, k:k + 1, :] = best
        col_pair[s_me, col_chunks + k:col_chunks + k + 1, :] = jnp.sum(total, axis=0, keepdims=True)
    x_cp[0]()
    x_cp[1]()
    g_first = -(math.log2(tgt_total) + merge(col_pair, n_s, col_chunks))
    base = jnp.exp2(jnp.concatenate(tops, axis=0) + g_first)
    b = base

    def row_products(slot, b):
        for c in range(row_chunks):
            total = tile[rows_of(c), rows_of(0)] * b[0:1, :]
            for k in range(1, col_chunks):
                total += tile[rows_of(c), rows_of(k)] * b[k:k + 1, :]
            row_sum[slot, t_me, c:c + 1, :] = jnp.sum(total.T, axis=0, keepdims=True)

    def add_up(buf, slot, n):
        total = buf[slot, 0]
        for d in range(1, n):
            total += buf[slot, d]
        return total

    for it in range(ITERS - 1):
        row_products(it, b)
        x_rs[it][0]()
        x_rs[it][1]()
        to_col(1.0 / (src_total * add_up(row_sum, it, n_t)))
        for k in range(col_chunks):
            total = jnp.zeros((8, LANES), f32)
            for c in range(row_chunks):
                e = tile[rows_of(c), rows_of(k)] * col[rows_of(c), :]
                total += jnp.sum(e.reshape(LANES // 8, 8, LANES), axis=0)
            col_sum[it, s_me, k:k + 1, :] = jnp.sum(total, axis=0, keepdims=True) * base[k:k + 1, :]
        x_cs[it][0]()
        x_cs[it][1]()
        beta = 1.0 / (tgt_total * add_up(col_sum, it, n_s))
        b = base * beta
    pot_ref[...] = EPS * (g_first * math.log(2.0) + jnp.log(beta))

    last = ITERS - 1
    for k in range(col_chunks):
        t_hi, t_lo = split(tgt_all[:, rows_of(k)] * b[k:k + 1, :])
        tgt_hi[:, rows_of(k)] = t_hi
        tgt_lo[:, rows_of(k)] = t_lo

    dims = (((1,), (1,)), ((), ()))

    def send_x(h, lo):
        return pltpu.make_async_remote_copy(
            src_ref=bary.at[pl.ds(pl.multiple_of((h * 2 + lo) * rows_own, 8), rows_own), :], dst_ref=from_x.at[h],
            send_sem=ax_s.at[h], recv_sem=ax_r.at[h], device_id=on_tgt(h_me * 2 + 1 - l_me), device_id_type=MESH)

    def send_z(h, sender):
        return pltpu.make_async_remote_copy(
            src_ref=to_z.at[h], dst_ref=from_z.at[sender], send_sem=bz_s.at[h], recv_sem=bz_r.at[sender],
            device_id=on_tgt(h * 2 + l_me), device_id_type=MESH)

    def own_rows(h):
        return bary[pl.ds(pl.multiple_of((h * 2 + l_me) * rows_own, 8), rows_own), :]

    def compute(h):
        product(h, 0)
        send_x(h, 1 - l_me).start()

    def product(h, lo):
        rows = pl.ds(pl.multiple_of(h * pair, 16), pair)
        e_hi, e_lo = split(tile[rows, :])
        out = lax.dot_general(e_hi, tgt_hi[...], dims, preferred_element_type=f32)
        out += lax.dot_general(e_hi, tgt_lo[...], dims, preferred_element_type=f32)
        out += lax.dot_general(e_lo, tgt_hi[...], dims, preferred_element_type=f32)
        bary[rows, :] = out

    def pass_on(h):
        send_x(h, 1 - l_me).wait_recv()
        to_z[h] = own_rows(h) + from_x[h]
        send_z(h, h_me).start()

    order = sorted(range(1, halves_t), key=lambda off: abs(2 * off - halves_t)) + [halves_t]
    for at, off in enumerate(order):
        compute(lax.rem(h_me + off, halves_t))
        if at == 0:
            row_products(last, b)
            x_rs[last][0]()
        else:
            pass_on(lax.rem(h_me + order[at - 1], halves_t))
    x_rs[last][1]()
    to_col(1.0 / add_up(row_sum, last, n_t))
    send_x(h_me, 1 - l_me).wait_recv()
    total = own_rows(h_me) + from_x[h_me]
    for off in range(1, halves_t):
        h = lax.rem(h_me + off, halves_t)
        send_z(h, h).wait_recv()
        total += from_z[h]
    inv = col[pl.ds(pl.multiple_of(t_me * rows_own, 8), rows_own), :]
    inv = jnp.concatenate([inv] * (feat // LANES), axis=1)
    vel_ref[...] = total * inv - noise_ref[...]

    drain_src()
    g_tgt[3]()
    for ops in [x_rp, x_cp] + x_rs + x_cs:
        ops[2]()
    for off in range(1, halves_t):
        h = lax.rem(h_me + off, halves_t)
        send_x(h, 1 - l_me).wait_send()
        send_z(h, h_me).wait_send()
    send_x(h_me, 1 - l_me).wait_send()


def per_device(n_s, n_t, noise, data):
    rows_own, feat = noise.shape
    n_rows, n_cols = rows_own * n_t, data.shape[0]
    rc, cc = n_rows // LANES, n_cols // LANES
    nh, nhs = n_t // 2, n_s // 2
    f32, bf16 = jnp.float32, jnp.bfloat16
    vmem = pltpu.VMEM
    dma = pltpu.SemaphoreType.DMA
    vel, pot = pl.pallas_call(
        functools.partial(kernel, n_s, n_t),
        out_shape=(jax.ShapeDtypeStruct((rows_own, feat), f32), jax.ShapeDtypeStruct((cc, LANES), f32)),
        in_specs=[pl.BlockSpec(memory_space=vmem)] * 2,
        out_specs=(pl.BlockSpec(memory_space=vmem), pl.BlockSpec(memory_space=vmem)),
        scratch_shapes=[
            vmem((n_rows, feat), f32), vmem((feat, n_cols), f32),
            vmem((feat, n_cols), bf16), vmem((feat, n_cols), bf16),
            vmem((n_rows, n_cols), f32), vmem((n_rows, LANES), f32), vmem((n_rows, feat), f32),
            vmem((n_t, 2 * rc, LANES), f32), vmem((n_s, 2 * cc, LANES), f32),
            vmem((ITERS, n_t, rc, LANES), f32), vmem((ITERS - 1, n_s, cc, LANES), f32),
            vmem((nh, rows_own, feat), f32), vmem((nh, rows_own, feat), f32), vmem((nh, rows_own, feat), f32),
            dma((nh,)), dma((nh,)), dma((nh,)), dma((nh,)), dma((nh,)),
            dma((nhs,)), dma((nhs,)), dma((nhs,)), dma((nhs,)),
            dma((n_t,)), dma((n_t,)), dma((n_s,)), dma((n_s,)),
            dma((ITERS, n_t)), dma((ITERS, n_t)), dma((ITERS - 1, n_s)), dma((ITERS - 1, n_s)),
            dma((nh,)), dma((nh,)), dma((nh,)), dma((nh,)),
        ],
        compiler_params=pltpu.CompilerParams(
            collective_id=0, has_side_effects=True, vmem_limit_bytes=48 * 1024 * 1024),
    )(noise, data.T)
    return vel, pot.reshape(n_cols)


def solution(mesh):
    return jax.shard_map(
        functools.partial(per_device, mesh.shape["src"], mesh.shape["tgt"]),
        mesh=mesh,
        in_specs=(P(("src", "tgt"), None), P("tgt", "src")),
        out_specs=(P(("src", "tgt"), None), P("tgt")),
        check_vma=False,
    )
```
